1024 devices in a mesh: seq: 16 (over y, core), exp: 16 (over x_lo, z), rep: 4 (over x_hi).
Axes of the slice: x: 8 (x_hi: 4, x_lo: 2; x = x_hi * 2 + x_lo), y: 8, z: 8, core: 2. Of those that a mesh axis runs over, the one named last changes fastest.
Arguments:
- queries: bfloat16 [2048, 6144], P('seq'), may hold values from -80 to 80
- keys: bfloat16 [2048, 1024], P('seq'), may hold values from -4.2 to 4.2
- values: bfloat16 [2048, 1024], P('seq'), may hold values from -6.2 to 6.2
- lengths: int32 [16], replicated, may hold values from 1 to 256, 2048 in all
- expert_ids: int32 [2048, 4], P('seq'), may hold values from 0 to 15, all different within a row; in each aligned block of 128 rows (0 to 127, 128 to 255, ...) at most 34 rows name the same one
- gate_share: float32 [2048, 4], P('seq'), may hold values from 0.2 to 1
- gate_up: bfloat16 [16, 6144, 2, 5376], P('exp', 'rep', None, 'seq'), may hold values from -0.15625 to 0.15625
- down_t: bfloat16 [16, 6144, 5376], P('exp', 'rep', 'seq'), may hold values from -0.15625 to 0.15625
Outputs:
- moe_out: bfloat16 [2048, 6144], P(('seq', 'exp'), 'rep')
The draws below stay inside these ranges and needn't reach their ends.
Inputs may be any that keep to these rules, and one draw needn't show every extreme that they name: The lengths sum to 2048; each is at most 256, and one is exactly 256. `expert_ids`: each token names 4 different experts. Among the 128 tokens of one device (aligned blocks of 128 positions), no expert is named more than 34 times, a bound that some block reaches.
All inputs are finite; a program needn't handle non-finite values.
Results may differ from the reference program's by a relative error of at most 0.035.
Values may be sent and summed in bfloat16 or wider, within the bound.
No kernel may reach another device: no remote copies, remote signals or barrier semaphores. Data moves between devices by JAX's collectives and lax.ppermute only.
A program may use at most 64 MiB of HBM per device.

```python
import math
import jax
import jax.numpy as jnp
import numpy as np
from jax import lax

HEADS = 48
KV = 8
HD = 128
EXPERTS = 16
TOPK = 4
FFW = 5376
TOK_DEV = 128
REACH = 2
DOC_MOST = 256
D = 6144
L = 2048
DOCS = 16
CAP = 34
N_SEQ = 16
N_EXP = 16
N_REP = 4


def drawn_keys(key):
    first = jax.random.fold_in(key, 0)
    rows = jnp.clip(jax.random.normal(first, (L, KV, HD), jnp.float32), -4.0, 4.0)
    return rows


def draw_keys(key, part):
    rows = drawn_keys(key)
    return rows.reshape(L, KV * HD).astype(jnp.bfloat16)


def draw_queries(key, part):
    key = jax.random.fold_in(key, 5)
    base = jnp.clip(jax.random.normal(key, (L, KV, HEADS // KV, HD), jnp.float32), -4.0, 4.0)
    return base.reshape(L, HEADS * HD).astype(jnp.bfloat16)


def draw_values(key, part):
    key = jax.random.fold_in(key, 17)
    first, second = jax.random.split(key, 2)
    common = 0.7 * jnp.clip(jax.random.normal(first, (KV * HD,), jnp.float32), -3.0, 3.0)
    noise = jnp.clip(jax.random.normal(second, (L, KV * HD), jnp.float32), -4.0, 4.0)
    return (common[None, :] + noise).astype(jnp.bfloat16)


def shard_levels(key, extent, pieces, smallest, high):
    level, own = 1.0, jax.random.fold_in(key, 6)
    for axis_at, blocks in pieces:
        steps = jnp.exp(jax.random.uniform(jax.random.fold_in(own, axis_at), (blocks,), jnp.float32, smallest / len(pieces), high / len(pieces)))
        level = level * jnp.repeat(steps, extent[axis_at] // blocks).reshape([-1 if axis == axis_at else 1 for axis in range(len(extent))])
    return level


def split_up(count, total, limit, skew):
    portions = [(1 << 20) // math.isqrt(grade ** skew) + 1 for grade in range(2, count + 1)]
    rest, holding = total - limit - (count - 1), [1] * (count - 1)
    while rest > 0:
        candidates = [i for i in range(count - 1) if holding[i] < limit]
        whole, left = sum([portions[i] for i in candidates]), rest
        for i in candidates:
            extra = min(limit - holding[i], max(1, left * portions[i] // whole), rest)
            holding[i] = holding[i] + extra
            rest = rest - extra
    return np.array([limit] + holding)


def ragged_sizes(stream_key, number_of, total, reach, slope):
    if number_of == 2:
        one = jax.random.randint(stream_key, (), max(1, total - reach), min(reach, total - 1) + 1)
        return jnp.stack([one, total - one])
    sizes = jnp.asarray(split_up(number_of, total, reach, slope), jnp.int32)
    twos = (number_of - 1) // 2
    source_of, receiver = sizes[1:1 + 2 * twos:2], sizes[2:2 + 2 * twos:2]
    margin = jnp.minimum(source_of - 1, reach - receiver)
    shifted = jax.random.randint(jax.random.fold_in(stream_key, 1), (twos,), 0, 1 << 20) % (margin + 1)
    sizes = sizes.at[1:1 + 2 * twos:2].set(source_of - shifted).at[2:2 + 2 * twos:2].set(receiver + shifted)
    return sizes[jax.random.permutation(jax.random.fold_in(stream_key, 2), number_of)]


def routed_block(key, own, number, rows, amount, top, most, slope):
    ranking = jax.random.permutation(key, amount)
    packed, usual = portions_of(amount, rows * top, most, slope, True), portions_of(amount, rows * top, most, slope, False)
    places = jnp.arange(amount)

    def named(tallies, turn):
        used = int((tallies > 0).sum())
        fixed = max(1, used // 4)
        moved = fixed + (places - fixed + turn * (used - fixed)) % max(1, amount - fixed)
        return jnp.zeros((amount,), jnp.int32).at[ranking[jnp.where(places < fixed, places, moved)]].set(jnp.asarray(tallies, jnp.int32))

    tallies = jnp.where(number % 4 == 0, named(packed, number // 4), named(usual, number - number // 4 - 1))
    mixed = jax.random.permutation(jax.random.fold_in(own, 3), amount)
    giver, receiver = mixed[0:amount // 2 * 2:2], mixed[1:amount // 2 * 2:2]
    room = jnp.minimum(tallies[giver] - 1, most - tallies[receiver]) // 2
    room = jnp.where((giver == ranking[0]) | (receiver == ranking[0]) | (tallies[receiver] == 0), 0, jnp.maximum(room, 0))
    moved = jax.random.randint(jax.random.fold_in(own, 4), (amount // 2,), 0, 1 << 20) % (room + 1)
    tallies = tallies.at[giver].add(-moved).at[receiver].add(moved)
    items = jnp.searchsorted(jnp.cumsum(tallies), jnp.arange(rows * top), side="right").astype(jnp.int32)
    table = items.reshape(top, rows).T
    table = table[jax.random.permutation(jax.random.fold_in(own, 1), rows)]
    turn = jax.random.randint(jax.random.fold_in(own, 2), (rows, 1), 0, top)
    return jnp.take_along_axis(table, (jnp.arange(top)[None, :] + turn) % top, axis=1)


def portions_of(number_of, total, most, lean, full):
    portions = [(1 << 20) // math.isqrt(standing ** lean) + 1 for standing in range(1, number_of + 1)]
    largest = most if full else min(most, max(-(-total // number_of), total * portions[0] // sum(portions)))
    least = 1 if total - largest >= number_of - 1 else 0
    given, spare = [largest] + [least] * (number_of - 1), total - largest - least * (number_of - 1)
    while spare > 0:
        movable = [i for i in range(1, number_of) if given[i] < largest] or [i for i in range(1, number_of) if given[i] < most]
        whole, budget = sum([portions[i] for i in movable]), spare
        for i in movable:
            more = min(most - given[i], max(1, budget * portions[i] // whole), spare)
            given[i] = given[i] + more
            spare = spare - more
    return np.array(given)


def gaussian(key, shape, scale, limit, cuts=(), held_as=jnp.bfloat16):
    array = jax.random.normal(key, shape, jnp.float32) * scale
    if len(cuts) > 0:
        array = shard_levels(key, shape, cuts, -0.22, 0.18) * array
    return jnp.clip(array, min=-limit, max=limit).astype(held_as)


def setup_inputs(seed: int = 0) -> dict:
    seeds = jax.random.split(jax.random.key(seed), 9)
    queries = draw_queries(jax.random.fold_in(seeds[8], 71), 0)
    keys = draw_keys(jax.random.fold_in(seeds[8], 71), 0)
    values = draw_values(jax.random.fold_in(seeds[8], 71), 0)
    lengths = ragged_sizes(seeds[3], DOCS, L, DOC_MOST, 2).astype(jnp.int32)
    expert_ids_keys = jax.random.split(jax.random.fold_in(seeds[4], 1), L // TOK_DEV)
    expert_ids_turns = jax.random.permutation(jax.random.fold_in(seeds[4], 3), L // TOK_DEV)
    expert_ids = jax.vmap(lambda own, number: routed_block(jax.random.fold_in(seeds[4], 2), own, number, TOK_DEV, EXPERTS, TOPK, CAP, 2))(expert_ids_keys, expert_ids_turns).reshape((L, TOPK))
    gate_share = jnp.clip(0.2 + 0.8 * jax.random.uniform(seeds[5], (L, TOPK), jnp.float32) ** shard_levels(seeds[5], (L, TOPK), ((0, 16),), -0.2, 0.2), 0.2, 1.0)
    gate_up = gaussian(seeds[6], (EXPERTS, D, 2, FFW), (D // 4) ** -0.5, 0.15625, ((0, 16), (1, 4), (3, 16)))
    down_t = gaussian(seeds[7], (EXPERTS, D, FFW), (FFW // 4) ** -0.5, 0.15625, ((0, 16), (1, 4), (2, 16)))
    return {"queries": queries, "keys": keys, "values": values, "lengths": lengths, "expert_ids": expert_ids, "gate_share": gate_share, "gate_up": gate_up, "down_t": down_t}


def segment_ids(lens, length):
    ends = jnp.cumsum(lens).astype(jnp.int32)
    places = jnp.arange(length, dtype=jnp.int32)
    return jnp.sum((places[:, None] >= ends[None, :]).astype(jnp.int32), axis=1)


def earlier(blocks_arr, back, fill):
    padding = jnp.full((back,) + blocks_arr.shape[1:], fill, blocks_arr.dtype)
    return jnp.concatenate([padding, blocks_arr[:blocks_arr.shape[0] - back]], 0)


def widen(blocks_arr, fill):
    parts = [earlier(blocks_arr, back, fill) for back in range(REACH, 0, -1)]
    return jnp.concatenate(parts + [blocks_arr], 1)


def attend(query, key_rows, value_rows, lens):
    segment = segment_ids(lens, L)
    tiles = L // TOK_DEV
    group = HEADS // KV
    q_tile = query.reshape(tiles, TOK_DEV, KV, group, HD).astype(jnp.float32)
    k_wide = widen(key_rows.reshape(tiles, TOK_DEV, KV, HD).astype(jnp.float32), 0.0)
    v_wide = widen(value_rows.reshape(tiles, TOK_DEV, KV, HD).astype(jnp.float32), 0.0)
    seg_tile = segment.reshape(tiles, TOK_DEV)
    seg_keys = widen(seg_tile, -1)
    q_pos = jnp.arange(L, dtype=jnp.int32).reshape(tiles, TOK_DEV)
    k_pos = q_pos[:, :1] - REACH * TOK_DEV + jnp.arange((REACH + 1) * TOK_DEV, dtype=jnp.int32)[None, :]
    allowed = (seg_tile[:, :, None] == seg_keys[:, None, :]) & (k_pos[:, None, :] <= q_pos[:, :, None])
    scores = jnp.einsum("ntsjd,nksd->nsjtk", q_tile, k_wide) * (HD ** -0.5)
    scores = jnp.where(allowed[:, None, None], scores, -jnp.inf)
    top = jnp.max(scores, axis=-1, keepdims=True)
    weights = jnp.exp(scores - top)
    probs = (weights / jnp.sum(weights, axis=-1, keepdims=True)).astype(jnp.bfloat16)
    out = jnp.einsum("nsjtk,nksd->ntsjd", probs.astype(jnp.float32), v_wide)
    return out.astype(jnp.bfloat16).reshape(L, HEADS * HD)


def one_expert(padded, index, shares, w_gate_up, w_down):
    rows = N_SEQ * CAP
    taken = padded[index].astype(jnp.float32).reshape(rows, N_REP, D // N_REP)
    weight = w_gate_up.astype(jnp.float32).reshape(N_REP, D // N_REP, 2 * FFW)
    parts = jnp.einsum("rbd,bdf->brf", taken, weight)
    parts = lax.optimization_barrier(parts.astype(jnp.bfloat16)).astype(jnp.float32)
    both = jnp.sum(parts, axis=0)
    hidden = (jax.nn.silu(both[:, :FFW]) * both[:, FFW:]).astype(jnp.bfloat16)
    hid = hidden.astype(jnp.float32).reshape(rows, N_SEQ, FFW // N_SEQ)
    down = w_down.astype(jnp.float32).reshape(D, N_SEQ, FFW // N_SEQ)
    outs = jnp.einsum("rsf,dsf->srd", hid, down)
    outs = lax.optimization_barrier(outs.astype(jnp.bfloat16)).astype(jnp.float32)
    expert_out = jnp.sum(outs, axis=0)
    return jnp.zeros((L + 1, D), jnp.float32).at[index].add(shares[:, None] * expert_out)


def reference(queries, keys, values, lengths, expert_ids, gate_share, gate_up, down_t):
    attended = attend(queries, keys, values, lengths)
    blocks = L // TOK_DEV
    ids = expert_ids.reshape(blocks, TOK_DEV * TOPK)
    onehot = (ids[:, :, None] == jnp.arange(EXPERTS, dtype=jnp.int32)[None, None, :]).astype(jnp.int32)
    before = (jnp.cumsum(onehot, axis=1) - onehot).astype(jnp.int32)
    slot = jnp.sum(before * onehot, axis=2).astype(jnp.int32)
    block_of = jnp.arange(blocks, dtype=jnp.int32)[:, None]
    dest = (ids * (blocks * CAP) + block_of * CAP + slot).reshape(-1).astype(jnp.int32)
    token_of = (jnp.arange(L * TOPK, dtype=jnp.int32) // TOPK).astype(jnp.int32)
    inverse = jnp.full((EXPERTS * blocks * CAP,), L, jnp.int32).at[dest].set(token_of)
    share_at = jnp.zeros((EXPERTS * blocks * CAP,), jnp.float32).at[dest].set(gate_share.reshape(-1))
    own = EXPERTS // N_EXP
    inverse = inverse.reshape(N_EXP, own, blocks * CAP)
    share_at = share_at.reshape(N_EXP, own, blocks * CAP)
    w_gate_up = gate_up.reshape(N_EXP, own, D, 2 * FFW)
    w_down = down_t.reshape(N_EXP, own, D, FFW)
    padded = jnp.concatenate([attended, jnp.zeros((1, D), jnp.bfloat16)], 0)

    def one_owner(total, inputs):
        index, shares, weight_a, weight_b = inputs
        term = jnp.zeros((L + 1, D), jnp.float32)
        for member in range(own):
            term = term + one_expert(padded, index[member], shares[member], weight_a[member], weight_b[member])
        term = lax.optimization_barrier(term[:L].astype(jnp.bfloat16)).astype(jnp.float32)
        return total + term, None

    total = jnp.zeros((L, D), jnp.float32)
    total, _ = lax.scan(one_owner, total, (inverse, share_at, w_gate_up, w_down))
    return total.astype(jnp.bfloat16)
```

```python
import functools

import jax
import jax.numpy as jnp
from jax import lax
from jax.experimental import pallas as pl
from jax.experimental.pallas import tpu as pltpu
from jax.sharding import PartitionSpec as P

HEADS = 48
KV = 8
HD = 128
REACH = 2
CAP = 34
MAIN = 32
LEFT = CAP - MAIN
SLOTS = 48
BF = jnp.bfloat16
F32 = jnp.float32
NT = (((1,), (1,)), ((), ()))


def dot(a, b):
    return jnp.dot(a, b, preferred_element_type=F32)


def iota(shape, dim):
    return lax.broadcasted_iota(jnp.int32, shape, dim)


def attend_kernel(heads, kv_heads, q_ref, far_ref, near_ref, own_ref, low_ref, high_ref, out_ref):
    group = heads // kv_heads
    rows = group * SLOTS
    left_rows = out_ref.shape[1] - heads * MAIN
    keys_in = (REACH + 1) * own_ref.shape[0]
    key_at = iota((rows, keys_in), 1)
    allowed = (key_at >= low_ref[...]) & (key_at <= high_ref[...])
    left = jnp.zeros((left_rows, HD), F32)
    for g in range(kv_heads):
        k_cols = slice(g * HD, (g + 1) * HD)
        v_cols = slice((kv_heads + g) * HD, (kv_heads + g + 1) * HD)
        k = jnp.concatenate([ref[:, k_cols] for ref in (far_ref, near_ref, own_ref)], 0)
        v = jnp.concatenate([ref[:, v_cols] for ref in (far_ref, near_ref, own_ref)], 0)
        q = jnp.concatenate([q_ref[:, (g * group + j) * HD : (g * group + j + 1) * HD] for j in range(group)], 0)
        scores = lax.dot_general(q, k, NT, preferred_element_type=F32) * HD ** (-0.5)
        scores = jnp.where(allowed, scores, -jnp.inf)
        weights = jnp.exp(scores - jnp.max(scores, axis=1, keepdims=True))
        probs = (weights / jnp.sum(weights, axis=1, keepdims=True)).astype(BF)
        mixed = dot(probs, v).astype(BF)
        for j in range(group):
            head = g * group + j
            part = mixed[j * SLOTS : j * SLOTS + MAIN]
            for y in range(out_ref.shape[0]):
                out_ref[y, head * MAIN : (head + 1) * MAIN, :] = part
        at = iota((left_rows, rows), 0) - g * group * LEFT
        col = iota((left_rows, rows), 1)
        wanted = (at >> 1) * SLOTS + MAIN + (at & 1)
        pick = ((col == wanted) & (at >= 0) & (at < group * LEFT)).astype(F32).astype(BF)
        left = left + dot(pick, mixed)
    left = left.astype(BF)
    for y in range(out_ref.shape[0]):
        out_ref[y, heads * MAIN :, :] = left


def left_index(shape, heads, blocks, left_rows, row_dim):
    row, col = iota(shape, row_dim), iota(shape, 1 - row_dim)
    per = blocks * LEFT
    head = row // per
    inside = row - head * per
    return (col == (inside >> 1) * left_rows + head * LEFT + (inside & 1)).astype(F32).astype(BF)


def gate_kernel(heads, own_ref, sib_ref, w_ref, out_ref, x_ref):
    blocks, flat, _ = own_ref.shape
    left_rows = flat - heads * MAIN
    main, extra = blocks * MAIN, blocks * LEFT
    halves = out_ref.shape[0] // 2
    pick = left_index((heads * extra, blocks * left_rows), heads, blocks, left_rows, 0)
    for half, ref in enumerate((own_ref, sib_ref)):
        for h in range(heads):
            x_ref[:main, h * HD : (h + 1) * HD] = ref[:, h * MAIN : (h + 1) * MAIN, :].reshape(main, HD)
        left = dot(pick, ref[:, heads * MAIN :, :].reshape(blocks * left_rows, HD)).astype(BF)
        for h in range(heads):
            x_ref[main:, h * HD : (h + 1) * HD] = left[h * extra : (h + 1) * extra]
        x = x_ref[...]
        for part in range(2):
            both = lax.dot_general(x, w_ref[0, part], NT, preferred_element_type=F32)
            m, n = main // halves, extra // halves
            for j in range(halves):
                rows = jnp.concatenate([both[j * m : (j + 1) * m], both[main + j * n : main + (j + 1) * n]], 0)
                out_ref[half * halves + j, part] = rows.astype(BF)


def hidden_kernel(in_ref, out_ref):
    n = in_ref.shape[0]
    gate = sum(in_ref[i, 0].astype(F32) for i in range(n))
    up = sum(in_ref[i, 1].astype(F32) for i in range(n))
    hidden = (gate / (1.0 + jnp.exp(-gate)) * up).astype(BF)
    for i in range(n):
        out_ref[i] = hidden


def down_kernel(heads, hid_ref, w_ref, own_ref, sib_ref):
    blocks, flat, _ = own_ref.shape
    left_rows = flat - heads * MAIN
    main, extra = blocks * MAIN, blocks * LEFT
    halves = hid_ref.shape[0] // 2
    m = main // halves
    put = left_index((blocks * left_rows, heads * extra), heads, blocks, left_rows, 1)
    for half, ref in enumerate((own_ref, sib_ref)):
        chunks = [hid_ref[half * halves + j].astype(F32) for j in range(halves)]
        hidden = jnp.concatenate([c[:m] for c in chunks] + [c[m:] for c in chunks], 0).astype(BF)
        out = dot(hidden, w_ref[0]).astype(BF)
        for h in range(heads):
            ref[:, h * MAIN : (h + 1) * MAIN, :] = out[:main, h * HD : (h + 1) * HD].reshape(blocks, MAIN, HD)
        stack = jnp.concatenate([out[main:, h * HD : (h + 1) * HD] for h in range(heads)], 0)
        ref[:, heads * MAIN :, :] = dot(put, stack).astype(BF).reshape(blocks, left_rows, HD)


def owner_kernel(heads, in_ref, put_ref, share_ref, left_share_ref, out_ref, x_ref):
    flat = in_ref.shape[1]
    left_rows = flat - heads * MAIN
    total = sum(in_ref[y].astype(F32) for y in range(in_ref.shape[0]))
    share = share_ref[...]
    left = (total[heads * MAIN :] * left_share_ref[...]).astype(BF)
    rest = SLOTS - MAIN
    row, col = iota((heads * rest, left_rows), 0), iota((heads * rest, left_rows), 1)
    head = row // rest
    inside = row - head * rest
    pick = ((col == head * LEFT + inside) & (inside < LEFT)).astype(F32).astype(BF)
    left = dot(pick, left).astype(BF)
    for h in range(heads):
        cols = slice(h * HD, (h + 1) * HD)
        x_ref[:MAIN, cols] = (total[h * MAIN : (h + 1) * MAIN] * share).astype(BF)
        x_ref[MAIN:, cols] = left[h * rest : (h + 1) * rest]
    out_ref[...] = dot(put_ref[...], x_ref[...]).astype(BF)


def call(kernel, shapes, scratch=(), flops=0, moved=0):
    return pl.pallas_call(
        kernel,
        out_shape=shapes,
        scratch_shapes=list(scratch),
        compiler_params=pltpu.CompilerParams(vmem_limit_bytes=48 * 1024 * 1024),
        cost_estimate=pl.CostEstimate(flops=flops, bytes_accessed=moved, transcendentals=0),
    )


def per_device(queries, keys, values, lengths, expert_ids, gate_share, gate_up, down_t):
    n_seq, n_exp, n_rep = (lax.axis_size(a) for a in ("seq", "exp", "rep"))
    tok = queries.shape[0]
    cols = gate_up.shape[1]
    hid = gate_up.shape[3]
    heads, kv_heads = cols // HD, KV // n_rep
    group = heads // kv_heads
    n_y = n_seq // 2
    left_rows = -(-heads * LEFT // 16) * 16
    flat = heads * MAIN + left_rows
    seq_at, exp_at, rep_at = (lax.axis_index(a) for a in ("seq", "exp", "rep"))
    same_core = [[2 * y + c for y in range(n_y)] for c in range(2)]
    sibling = [(i, i ^ 1) for i in range(n_seq)]

    kv_cols = kv_heads * HD
    kv = jnp.concatenate(
        [
            lax.dynamic_slice_in_dim(keys, rep_at * kv_cols, kv_cols, 1),
            lax.dynamic_slice_in_dim(values, rep_at * kv_cols, kv_cols, 1),
        ],
        1,
    )
    far = lax.ppermute(kv, "seq", [(i, (i + 2) % n_seq) for i in range(n_seq)])
    near = lax.ppermute(kv, "seq", [(i, (i + 1) % n_seq) for i in range(n_seq)])

    hit = expert_ids == exp_at
    match = jnp.any(hit, axis=1).astype(jnp.int32)
    share_of = jnp.sum(jnp.where(hit, gate_share, 0.0), axis=1)
    rank = jnp.cumsum(match) - match
    slot = jnp.where(match > 0, rank, -1)
    pick = slot[None, :] == jnp.arange(SLOTS, dtype=jnp.int32)[:, None]
    put = (slot[:, None] == jnp.arange(SLOTS, dtype=jnp.int32)[None, :]).astype(BF)
    place = jnp.arange(tok, dtype=jnp.int32)
    ends = jnp.cumsum(lengths)
    starts = jnp.max(jnp.where(ends[None, :] <= seq_at * tok + place[:, None], ends[None, :], 0), axis=1)
    low_of = starts - (seq_at - REACH) * tok
    low = jnp.sum(jnp.where(pick, low_of[None, :], 0), axis=1)
    high = jnp.sum(jnp.where(pick, place[None, :], 0), axis=1) + REACH * tok
    share = jnp.sum(jnp.where(pick, share_of[None, :], 0.0), axis=1)
    left_share = jnp.tile(share[MAIN:CAP], left_rows // LEFT)
    q_cols = lax.dynamic_slice_in_dim(queries, rep_at * cols, cols, 1)
    q_rows = dot(pick.astype(BF), q_cols).astype(BF)

    spread = call(
        functools.partial(attend_kernel, heads, kv_heads),
        jax.ShapeDtypeStruct((n_y, flat, HD), BF),
        flops=4 * heads * SLOTS * 3 * tok * HD,
    )(q_rows, far, near, kv, jnp.tile(low, group)[:, None], jnp.tile(high, group)[:, None])

    own = lax.all_to_all(spread, "seq", split_axis=0, concat_axis=0, tiled=True, axis_index_groups=same_core)
    sib = lax.ppermute(own, "seq", sibling)

    rows = n_seq * CAP // n_rep
    gate_w = jnp.transpose(gate_up, (0, 2, 3, 1))
    down_w = jnp.transpose(down_t, (0, 2, 1))
    parts = call(
        functools.partial(gate_kernel, heads),
        jax.ShapeDtypeStruct((n_rep, 2, rows, hid), BF),
        [pltpu.VMEM((n_y * CAP, cols), BF)],
        flops=4 * n_seq * CAP * cols * hid,
    )(own, sib, gate_w)
    parts = lax.all_to_all(parts, "rep", split_axis=0, concat_axis=0, tiled=True)
    hidden = call(hidden_kernel, jax.ShapeDtypeStruct((n_rep, rows, hid), BF))(parts)
    hidden = lax.all_to_all(hidden, "rep", split_axis=0, concat_axis=0, tiled=True)
    mine, theirs = call(
        functools.partial(down_kernel, heads),
        [jax.ShapeDtypeStruct((n_y, flat, HD), BF)] * 2,
        flops=2 * n_seq * CAP * cols * hid,
    )(hidden, down_w)
    back = lax.ppermute(theirs, "seq", sibling)
    mine = (mine.astype(F32) + back.astype(F32)).astype(BF)
    mine = lax.all_to_all(mine, "seq", split_axis=0, concat_axis=0, tiled=True, axis_index_groups=same_core)
    term = call(
        functools.partial(owner_kernel, heads),
        jax.ShapeDtypeStruct((tok, cols), BF),
        [pltpu.VMEM((SLOTS, cols), BF)],
        flops=2 * SLOTS * tok * cols,
    )(mine, put, share[:MAIN, None], left_share[:, None])
    terms = lax.all_to_all(term.reshape(n_exp, tok // n_exp, cols), "exp", split_axis=0, concat_axis=0, tiled=True)
    return jnp.sum(terms.astype(F32), axis=0).astype(BF)


def solution(mesh):
    in_specs = (
        P("seq", None),
        P("seq", None),
        P("seq", None),
        P(),
        P("seq", None),
        P("seq", None),
        P("exp", "rep", None, "seq"),
        P("exp", "rep", "seq"),
    )
    return jax.shard_map(
        per_device, mesh=mesh, in_specs=in_specs, out_specs=P(("seq", "exp"), "rep"), check_vma=False
    )
```

```python
import functools

import jax
import jax.numpy as jnp
from jax import lax
from jax.experimental import pallas as pl
from jax.experimental.pallas import tpu as pltpu
from jax.sharding import PartitionSpec as P

HEADS = 48
KV = 8
HD = 128
REACH = 2
CAP = 34
MAIN = 32
LEFT = CAP - MAIN
SLOTS = 48
BF = jnp.bfloat16
F32 = jnp.float32
NT = (((1,), (1,)), ((), ()))


def dot(a, b):
    return jnp.dot(a, b, preferred_element_type=F32)


def iota(shape, dim):
    return lax.broadcasted_iota(jnp.int32, shape, dim)


def attend_kernel(heads, kv_heads, q_ref, far_ref, near_ref, own_ref, low_ref, high_ref, out_ref):
    group = heads // kv_heads
    rows = group * SLOTS
    left_rows = out_ref.shape[1] - heads * MAIN
    keys_in = (REACH + 1) * own_ref.shape[0]
    key_at = iota((rows, keys_in), 1)
    allowed = (key_at >= low_ref[...]) & (key_at <= high_ref[...])
    left = jnp.zeros((left_rows, HD), F32)
    for g in range(kv_heads):
        k_cols = slice(g * HD, (g + 1) * HD)
        v_cols = slice((kv_heads + g) * HD, (kv_heads + g + 1) * HD)
        k = jnp.concatenate([ref[:, k_cols] for ref in (far_ref, near_ref, own_ref)], 0)
        v = jnp.concatenate([ref[:, v_cols] for ref in (far_ref, near_ref, own_ref)], 0)
        q = jnp.concatenate([q_ref[:, (g * group + j) * HD : (g * group + j + 1) * HD] for j in range(group)], 0)
        scores = lax.dot_general(q, k, NT, preferred_element_type=F32) * HD ** (-0.5)
        scores = jnp.where(allowed, scores, -jnp.inf)
        weights = jnp.exp(scores - jnp.max(scores, axis=1, keepdims=True))
        probs = (weights / jnp.sum(weights, axis=1, keepdims=True)).astype(BF)
        mixed = dot(probs, v).astype(BF)
        for j in range(group):
            head = g * group + j
            part = mixed[j * SLOTS : j * SLOTS + MAIN]
            for y in range(out_ref.shape[0]):
                out_ref[y, head * MAIN : (head + 1) * MAIN, :] = part
        at = iota((left_rows, rows), 0) - g * group * LEFT
        col = iota((left_rows, rows), 1)
        wanted = (at >> 1) * SLOTS + MAIN + (at & 1)
        pick = ((col == wanted) & (at >= 0) & (at < group * LEFT)).astype(F32).astype(BF)
        left = left + dot(pick, mixed)
    left = left.astype(BF)
    for y in range(out_ref.shape[0]):
        out_ref[y, heads * MAIN :, :] = left


def left_index(shape, heads, blocks, left_rows, row_dim):
    row, col = iota(shape, row_dim), iota(shape, 1 - row_dim)
    per = blocks * LEFT
    head = row // per
    inside = row - head * per
    return (col == (inside >> 1) * left_rows + head * LEFT + (inside & 1)).astype(F32).astype(BF)


def own_of(shape, row_dim, n, per):
    row, col = iota(shape, row_dim), iota(shape, 1 - row_dim)
    chunk = row // (2 * per)
    inside = row - chunk * 2 * per
    shard = inside // per
    return (col == shard * n * per + chunk * per + inside - shard * per).astype(F32).astype(BF)


def gate_kernel(heads, in_ref, own_w_ref, sib_w_ref, out_ref, x_ref):
    blocks, flat, _ = in_ref.shape
    chunks = out_ref.shape[0]
    left_rows = flat - heads * MAIN
    main, extra = blocks * MAIN, blocks * LEFT
    m, n = main // chunks, extra // chunks
    pick = left_index((heads * extra, blocks * left_rows), heads, blocks, left_rows, 0)
    for h in range(heads):
        x_ref[:main, h * HD : (h + 1) * HD] = in_ref[:, h * MAIN : (h + 1) * MAIN, :].reshape(main, HD)
    left = dot(pick, in_ref[:, heads * MAIN :, :].reshape(blocks * left_rows, HD)).astype(BF)
    for h in range(heads):
        x_ref[main:, h * HD : (h + 1) * HD] = left[h * extra : (h + 1) * extra]
    x = x_ref[...]
    order = own_of((2 * extra, 2 * extra), 0, chunks, n)
    for part in range(2):
        own = lax.dot_general(x, own_w_ref[0, part], NT, preferred_element_type=F32)
        sib = lax.dot_general(x, sib_w_ref[0, part], NT, preferred_element_type=F32)
        left = dot(order, jnp.concatenate([own[main:], sib[main:]], 0).astype(BF))
        for j in range(chunks):
            rows = [own[j * m : (j + 1) * m], sib[j * m : (j + 1) * m], left[j * 2 * n : (j + 1) * 2 * n]]
            out_ref[j, part] = jnp.concatenate(rows, 0).astype(BF)


def hidden_kernel(in_ref, out_ref):
    n = in_ref.shape[0]
    gate = sum(in_ref[i, 0].astype(F32) for i in range(n))
    up = sum(in_ref[i, 1].astype(F32) for i in range(n))
    hidden = (gate / (1.0 + jnp.exp(-gate)) * up).astype(BF)
    for i in range(n):
        out_ref[i] = hidden


def down_kernel(heads, hid_ref, own_w_ref, sib_w_ref, out_ref):
    blocks, flat, _ = out_ref.shape
    chunks = hid_ref.shape[0]
    left_rows = flat - heads * MAIN
    main, extra = blocks * MAIN, blocks * LEFT
    m, n = main // chunks, extra // chunks
    put = left_index((blocks * left_rows, heads * extra), heads, blocks, left_rows, 1)
    held = [hid_ref[j].astype(F32) for j in range(chunks)]
    order = own_of((2 * extra, 2 * extra), 1, chunks, n)
    left = dot(order, jnp.concatenate([c[2 * m :] for c in held], 0).astype(BF))
    own = jnp.concatenate([c[:m] for c in held] + [left[:extra]], 0).astype(BF)
    sib = jnp.concatenate([c[m : 2 * m] for c in held] + [left[extra:]], 0).astype(BF)
    out = (dot(own, own_w_ref[0]) + dot(sib, sib_w_ref[0])).astype(BF)
    for h in range(heads):
        out_ref[:, h * MAIN : (h + 1) * MAIN, :] = out[:main, h * HD : (h + 1) * HD].reshape(blocks, MAIN, HD)
    stack = jnp.concatenate([out[main:, h * HD : (h + 1) * HD] for h in range(heads)], 0)
    out_ref[:, heads * MAIN :, :] = dot(put, stack).astype(BF).reshape(blocks, left_rows, HD)


def owner_kernel(heads, in_ref, put_ref, share_ref, left_share_ref, out_ref, x_ref):
    flat = in_ref.shape[1]
    left_rows = flat - heads * MAIN
    total = sum(in_ref[y].astype(F32) for y in range(in_ref.shape[0]))
    share = share_ref[...]
    left = (total[heads * MAIN :] * left_share_ref[...]).astype(BF)
    rest = SLOTS - MAIN
    row, col = iota((heads * rest, left_rows), 0), iota((heads * rest, left_rows), 1)
    head = row // rest
    inside = row - head * rest
    pick = ((col == head * LEFT + inside) & (inside < LEFT)).astype(F32).astype(BF)
    left = dot(pick, left).astype(BF)
    for h in range(heads):
        cols = slice(h * HD, (h + 1) * HD)
        x_ref[:MAIN, cols] = (total[h * MAIN : (h + 1) * MAIN] * share).astype(BF)
        x_ref[MAIN:, cols] = left[h * rest : (h + 1) * rest]
    out_ref[...] = dot(put_ref[...], x_ref[...]).astype(BF)


def call(kernel, shapes, scratch=(), flops=0, moved=0):
    return pl.pallas_call(
        kernel,
        out_shape=shapes,
        scratch_shapes=list(scratch),
        compiler_params=pltpu.CompilerParams(vmem_limit_bytes=48 * 1024 * 1024),
        cost_estimate=pl.CostEstimate(flops=flops, bytes_accessed=moved, transcendentals=0),
    )


def per_device(queries, keys, values, lengths, expert_ids, gate_share, gate_up, down_t):
    n_seq, n_exp, n_rep = (lax.axis_size(a) for a in ("seq", "exp", "rep"))
    tok = queries.shape[0]
    cols = gate_up.shape[1]
    hid = gate_up.shape[3]
    heads, kv_heads = cols // HD, KV // n_rep
    group = heads // kv_heads
    n_y = n_seq // 2
    left_rows = -(-heads * LEFT // 16) * 16
    flat = heads * MAIN + left_rows
    seq_at, exp_at, rep_at = (lax.axis_index(a) for a in ("seq", "exp", "rep"))
    same_core = [[2 * y + c for y in range(n_y)] for c in range(2)]
    sibling = [(i, i ^ 1) for i in range(n_seq)]

    kv_cols = kv_heads * HD
    kv = jnp.concatenate(
        [
            lax.dynamic_slice_in_dim(keys, rep_at * kv_cols, kv_cols, 1),
            lax.dynamic_slice_in_dim(values, rep_at * kv_cols, kv_cols, 1),
        ],
        1,
    )
    far = lax.ppermute(kv, "seq", [(i, (i + 2) % n_seq) for i in range(n_seq)])
    near = lax.ppermute(kv, "seq", [(i, (i + 1) % n_seq) for i in range(n_seq)])

    hit = expert_ids == exp_at
    match = jnp.any(hit, axis=1).astype(jnp.int32)
    share_of = jnp.sum(jnp.where(hit, gate_share, 0.0), axis=1)
    rank = jnp.cumsum(match) - match
    slot = jnp.where(match > 0, rank, -1)
    pick = slot[None, :] == jnp.arange(SLOTS, dtype=jnp.int32)[:, None]
    put = (slot[:, None] == jnp.arange(SLOTS, dtype=jnp.int32)[None, :]).astype(BF)
    place = jnp.arange(tok, dtype=jnp.int32)
    ends = jnp.cumsum(lengths)
    starts = jnp.max(jnp.where(ends[None, :] <= seq_at * tok + place[:, None], ends[None, :], 0), axis=1)
    low_of = starts - (seq_at - REACH) * tok
    low = jnp.sum(jnp.where(pick, low_of[None, :], 0), axis=1)
    high = jnp.sum(jnp.where(pick, place[None, :], 0), axis=1) + REACH * tok
    share = jnp.sum(jnp.where(pick, share_of[None, :], 0.0), axis=1)
    left_share = jnp.tile(share[MAIN:CAP], left_rows // LEFT)
    q_cols = lax.dynamic_slice_in_dim(queries, rep_at * cols, cols, 1)
    q_rows = dot(pick.astype(BF), q_cols).astype(BF)

    spread = call(
        functools.partial(attend_kernel, heads, kv_heads),
        jax.ShapeDtypeStruct((n_y, flat, HD), BF),
        flops=4 * heads * SLOTS * 3 * tok * HD,
    )(q_rows, far, near, kv, jnp.tile(low, group)[:, None], jnp.tile(high, group)[:, None])

    gate_w = jnp.transpose(gate_up, (0, 2, 3, 1))
    down_w = jnp.transpose(down_t, (0, 2, 1))
    sib_gate_w = lax.ppermute(gate_w, "seq", sibling)
    sib_down_w = lax.ppermute(down_w, "seq", sibling)
    mine = lax.all_to_all(spread, "seq", split_axis=0, concat_axis=0, tiled=True, axis_index_groups=same_core)

    rows = 2 * n_y * CAP // n_rep
    parts = call(
        functools.partial(gate_kernel, heads),
        jax.ShapeDtypeStruct((n_rep, 2, rows, hid), BF),
        [pltpu.VMEM((n_y * CAP, cols), BF)],
        flops=8 * n_y * CAP * cols * hid,
    )(mine, gate_w, sib_gate_w)
    parts = lax.all_to_all(parts, "rep", split_axis=0, concat_axis=0, tiled=True)
    hidden = call(hidden_kernel, jax.ShapeDtypeStruct((n_rep, rows, hid), BF))(parts)
    hidden = lax.all_to_all(hidden, "rep", split_axis=0, concat_axis=0, tiled=True)
    mine = call(
        functools.partial(down_kernel, heads),
        jax.ShapeDtypeStruct((n_y, flat, HD), BF),
        flops=4 * n_y * CAP * cols * hid,
    )(hidden, down_w, sib_down_w)
    mine = lax.all_to_all(mine, "seq", split_axis=0, concat_axis=0, tiled=True, axis_index_groups=same_core)
    term = call(
        functools.partial(owner_kernel, heads),
        jax.ShapeDtypeStruct((tok, cols), BF),
        [pltpu.VMEM((SLOTS, cols), BF)],
        flops=2 * SLOTS * tok * cols,
    )(mine, put, share[:MAIN, None], left_share[:, None])
    terms = lax.all_to_all(term.reshape(n_exp, tok // n_exp, cols), "exp", split_axis=0, concat_axis=0, tiled=True)
    return jnp.sum(terms.astype(F32), axis=0).astype(BF)


def solution(mesh):
    in_specs = (
        P("seq", None),
        P("seq", None),
        P("seq", None),
        P(),
        P("seq", None),
        P("seq", None),
        P("exp", "rep", None, "seq"),
        P("exp", "rep", "seq"),
    )
    return jax.shard_map(
        per_device, mesh=mesh, in_specs=in_specs, out_specs=P(("seq", "exp"), "rep"), check_vma=False
    )
```

```python
import functools

import jax
import jax.numpy as jnp
from jax import lax
from jax.experimental import pallas as pl
from jax.experimental.pallas import tpu as pltpu
from jax.sharding import PartitionSpec as P

HEADS = 48
KV = 8
HD = 128
REACH = 2
CAP = 34
MAIN = 32
LEFT = CAP - MAIN
SLOTS = 48
BF = jnp.bfloat16
F32 = jnp.float32
NT = (((1,), (1,)), ((), ()))


def dot(a, b):
    return jnp.dot(a, b, preferred_element_type=F32)


def iota(shape, dim):
    return lax.broadcasted_iota(jnp.int32, shape, dim)


def attend_kernel(heads, kv_heads, q_ref, far_ref, near_ref, own_ref, low_ref, high_ref, share_in, left_in, out_ref, share_ref, left_ref):
    share_ref[...] = share_in[...]
    left_ref[...] = left_in[...]
    group = heads // kv_heads
    rows = group * SLOTS
    left_rows = out_ref.shape[0] - heads * MAIN
    keys_in = (REACH + 1) * own_ref.shape[0]
    key_at = iota((rows, keys_in), 1)
    allowed = (key_at >= low_ref[...]) & (key_at <= high_ref[...])
    left = jnp.zeros((left_rows, HD), F32)
    for g in range(kv_heads):
        k_cols = slice(g * HD, (g + 1) * HD)
        v_cols = slice((kv_heads + g) * HD, (kv_heads + g + 1) * HD)
        k = jnp.concatenate([ref[:, k_cols] for ref in (far_ref, near_ref, own_ref)], 0)
        v = jnp.concatenate([ref[:, v_cols] for ref in (far_ref, near_ref, own_ref)], 0)
        q = jnp.concatenate([q_ref[:, (g * group + j) * HD : (g * group + j + 1) * HD] for j in range(group)], 0)
        scores = lax.dot_general(q, k, NT, preferred_element_type=F32) * HD ** (-0.5)
        scores = jnp.where(allowed, scores, -jnp.inf)
        weights = jnp.exp(scores - jnp.max(scores, axis=1, keepdims=True))
        probs = (weights / jnp.sum(weights, axis=1, keepdims=True)).astype(BF)
        mixed = dot(probs, v).astype(BF)
        for j in range(group):
            head = g * group + j
            out_ref[head * MAIN : (head + 1) * MAIN, :] = mixed[j * SLOTS : j * SLOTS + MAIN]
        at = iota((left_rows, rows), 0) - g * group * LEFT
        col = iota((left_rows, rows), 1)
        wanted = (at >> 1) * SLOTS + MAIN + (at & 1)
        pick = ((col == wanted) & (at >= 0) & (at < group * LEFT)).astype(F32).astype(BF)
        left = left + dot(pick, mixed)
    out_ref[heads * MAIN :, :] = left.astype(BF)


def left_index(shape, heads, blocks, left_rows, row_dim):
    row, col = iota(shape, row_dim), iota(shape, 1 - row_dim)
    per = blocks * LEFT
    head = row // per
    inside = row - head * per
    return (col == (inside >> 1) * left_rows + head * LEFT + (inside & 1)).astype(F32).astype(BF)


def joined(own, sib, start, stop):
    n = own.shape[0]
    parts = []
    if start < n:
        parts.append(own[start : min(stop, n)])
    if stop > n:
        parts.append(sib[max(start - n, 0) : stop - n])
    return parts[0] if len(parts) == 1 else jnp.concatenate(parts, 0)


def silu_times(gate, up):
    return gate / (1.0 + jnp.exp(-gate)) * up


def gate_kernel(heads, in_ref, own_w_ref, far_w_ref, out_ref, x_ref, sib_w_ref, sem):
    fetch = pltpu.make_async_copy(far_w_ref, sib_w_ref, sem)
    fetch.start()
    blocks, flat, _ = in_ref.shape
    chunks = out_ref.shape[0]
    left_rows = flat - heads * MAIN
    main, extra = blocks * MAIN, blocks * LEFT
    m, n = main // chunks, extra // chunks
    pick = left_index((heads * extra, blocks * left_rows), heads, blocks, left_rows, 0)
    for h in range(heads):
        x_ref[:main, h * HD : (h + 1) * HD] = in_ref[:, h * MAIN : (h + 1) * MAIN, :].reshape(main, HD)
    left = dot(pick, in_ref[:, heads * MAIN :, :].reshape(blocks * left_rows, HD)).astype(BF)
    for h in range(heads):
        x_ref[main:, h * HD : (h + 1) * HD] = left[h * extra : (h + 1) * extra]
    x = x_ref[...]
    full = 2 * own_w_ref.shape[2] // HD

    def times(*w):
        w = w[0] if len(w) == 1 else jnp.concatenate(w, 0)
        return lax.dot_general(x, w, NT, preferred_element_type=F32)

    def units(part, start, stop):
        return joined(own_w_ref.at[0, part], sib_w_ref.at[0, part], start, stop)

    tiles = [[], []]
    for t in range(0, full - 1, 2):
        if t == 2:
            fetch.wait()
        for part in range(2):
            both = times(units(part, t * HD, (t + 2) * HD))
            tiles[part] += [both[:, :HD], both[:, HD:]]
    both = times(*(units(part, (full - 1) * HD, full * HD) for part in range(2)))
    tiles[0].append(both[:, :HD])
    tiles[1].append(both[:, HD:])
    rest = [units(part, full * HD, full * HD + HD // 4) for part in range(2)]
    rest = times(*rest, *rest)
    tiles = tiles[0] + tiles[1]
    packed = 2 * full * m + m // 2
    stack = jnp.concatenate([t[main:] for t in tiles + [rest]], 0).astype(BF)
    per = out_ref.shape[1] - packed
    row, col = iota((chunks * per, stack.shape[0]), 0), iota((chunks * per, stack.shape[0]), 1)
    chunk = row // per
    inside = row - chunk * per
    t, up, i = inside // (2 * n), (inside // n) & 1, inside & (n - 1)
    wanted = jnp.where(t < full, (up * full + t) * extra, jnp.where(up == 0, 2 * full * extra, -stack.shape[0]))
    order = (col == wanted + chunk * n + i).astype(F32).astype(BF)
    left = dot(order, stack).astype(BF)
    first = iota((m // 2, HD), 1) < HD // 2
    for j in range(chunks):
        for k, tile in enumerate(tiles):
            out_ref[j, k * m : (k + 1) * m, :] = tile[j * m : (j + 1) * m].astype(BF)
        pair = jnp.where(first, rest[j * m : j * m + m // 2], rest[j * m + m // 2 : (j + 1) * m])
        out_ref[j, 2 * full * m : packed, :] = pair.astype(BF)
        out_ref[j, packed:, :] = left[j * per : (j + 1) * per]


def hidden_kernel(full, m, n, in_ref, out_ref):
    both = sum(in_ref[i].astype(F32) for i in range(in_ref.shape[0]))
    tall, packed = full * m, 2 * full * m + m // 2
    quarter = HD // 4

    def rest(x):
        return silu_times(x, pltpu.roll(x, HD - quarter, 1))

    main = silu_times(both[:tall], both[tall : 2 * tall])
    pair = both[2 * tall : packed]
    pair = jnp.where((iota(pair.shape, 1) & (2 * quarter - 1)) < quarter, rest(pair), 0.0)
    left = both[packed : packed + 2 * n * full]
    left = silu_times(left, pltpu.roll(left, left.shape[0] - n, 0))
    last = both[packed + 2 * n * full :]
    last = jnp.where(iota(last.shape, 1) < quarter, rest(last), 0.0)
    left = jnp.concatenate([left, last], 0).astype(BF)
    rows = out_ref.shape[0] - tall - m // 2
    row, col = iota((rows, left.shape[0]), 0), iota((rows, left.shape[0]), 1)
    pick = ((col == row // n * 2 * n + (row & (n - 1))) & (row < n * (full + 1))).astype(F32).astype(BF)
    out_ref[:tall, :] = main.astype(BF)
    out_ref[tall : tall + m // 2, :] = pair.astype(BF)
    out_ref[tall + m // 2 :, :] = dot(pick, left).astype(BF)


def down_kernel(heads, hid_ref, own_w_ref, sib_w_ref, out_ref):
    blocks, flat, _ = out_ref.shape
    chunks = hid_ref.shape[0]
    left_rows = flat - heads * MAIN
    main, extra = blocks * MAIN, blocks * LEFT
    m, n = main // chunks, extra // chunks
    put = left_index((blocks * left_rows, heads * extra), heads, blocks, left_rows, 1)
    full = 2 * own_w_ref.shape[1] // HD
    tall = full * m
    rest_rows = hid_ref.shape[1] - tall - m // 2
    tiles = [jnp.concatenate([hid_ref[j, t * m : (t + 1) * m, :] for j in range(chunks)], 0) for t in range(full)]
    first = iota((m // 2, HD), 1) < HD // 2
    pairs = []
    for j in range(chunks):
        pair = hid_ref[j, tall : tall + m // 2, :].astype(F32)
        pairs += [jnp.where(first, pair, 0.0), jnp.where(first, 0.0, pair)]
    tiles.append(jnp.concatenate(pairs, 0).astype(BF))
    stack = jnp.concatenate([hid_ref[j, tall + m // 2 :, :] for j in range(chunks)], 0)
    shape = ((full + 1) * extra, stack.shape[0])
    row, col = iota(shape, 0), iota(shape, 1)
    t = row // extra
    inside = row - t * extra
    order = (col == inside // n * rest_rows + t * n + (inside & (n - 1))).astype(F32).astype(BF)
    left = dot(order, stack).astype(BF)
    hidden = [jnp.concatenate([tile, left[t * extra : (t + 1) * extra]], 0) for t, tile in enumerate(tiles)]

    def units(start, stop):
        return joined(own_w_ref.at[0], sib_w_ref.at[0], start, stop)

    out = None
    for t in range(0, full + 1, 2):
        if t + 2 <= full:
            w = units(t * HD, (t + 2) * HD)
        else:
            w = jnp.concatenate([units(t * HD, full * HD)] + [units(full * HD, full * HD + HD // 4)] * 4, 0)
        term = dot(jnp.concatenate(hidden[t : t + 2], 1), w)
        out = term if out is None else out + term
    out = out.astype(BF)
    for h in range(heads):
        out_ref[:, h * MAIN : (h + 1) * MAIN, :] = out[:main, h * HD : (h + 1) * HD].reshape(blocks, MAIN, HD)
    stack = jnp.concatenate([out[main:, h * HD : (h + 1) * HD] for h in range(heads)], 0)
    out_ref[:, heads * MAIN :, :] = dot(put, stack).astype(BF).reshape(blocks, left_rows, HD)


def owner_kernel(heads, in_ref, put_ref, share_ref, left_share_ref, out_ref, x_ref):
    flat = in_ref.shape[1]
    left_rows = flat - heads * MAIN
    total = sum(in_ref[y].astype(F32) for y in range(in_ref.shape[0]))
    share = share_ref[...]
    left = (total[heads * MAIN :] * left_share_ref[...]).astype(BF)
    rest = SLOTS - MAIN
    row, col = iota((heads * rest, left_rows), 0), iota((heads * rest, left_rows), 1)
    head = row // rest
    inside = row - head * rest
    pick = ((col == head * LEFT + inside) & (inside < LEFT)).astype(F32).astype(BF)
    left = dot(pick, left).astype(BF)
    for h in range(heads):
        cols = slice(h * HD, (h + 1) * HD)
        x_ref[:MAIN, cols] = (total[h * MAIN : (h + 1) * MAIN] * share).astype(BF)
        x_ref[MAIN:, cols] = left[h * rest : (h + 1) * rest]
    out_ref[...] = dot(put_ref[...], x_ref[...]).astype(BF)


def call(kernel, shapes, scratch=(), flops=0, moved=0, in_hbm=None):
    spaces = {}
    if in_hbm is not None:
        spaces["in_specs"] = [pl.BlockSpec(memory_space=pl.ANY if at == in_hbm[0] else pltpu.VMEM) for at in range(in_hbm[1])]
    return pl.pallas_call(
        kernel,
        **spaces,
        out_shape=shapes,
        scratch_shapes=list(scratch),
        compiler_params=pltpu.CompilerParams(vmem_limit_bytes=12 * 1024 * 1024),
        cost_estimate=pl.CostEstimate(flops=flops, bytes_accessed=moved, transcendentals=0),
    )


def per_device(queries, keys, values, lengths, expert_ids, gate_share, gate_up, down_t):
    n_seq, n_exp, n_rep = (lax.axis_size(a) for a in ("seq", "exp", "rep"))
    tok = queries.shape[0]
    cols = gate_up.shape[1]
    hid = gate_up.shape[3]
    heads, kv_heads = cols // HD, KV // n_rep
    group = heads // kv_heads
    n_y = n_seq // 2
    left_rows = -(-heads * LEFT // 16) * 16
    flat = heads * MAIN + left_rows
    seq_at, exp_at, rep_at = (lax.axis_index(a) for a in ("seq", "exp", "rep"))
    same_core = [[2 * y + c for y in range(n_y)] for c in range(2)]
    sibling = [(i, i ^ 1) for i in range(n_seq)]

    kv_cols = kv_heads * HD
    kv = jnp.concatenate(
        [
            lax.dynamic_slice_in_dim(keys, rep_at * kv_cols, kv_cols, 1),
            lax.dynamic_slice_in_dim(values, rep_at * kv_cols, kv_cols, 1),
        ],
        1,
    )
    far = lax.ppermute(kv, "seq", [(i, (i + 2) % n_seq) for i in range(n_seq)])
    near = lax.ppermute(kv, "seq", [(i, (i + 1) % n_seq) for i in range(n_seq)])

    hit = expert_ids == exp_at
    match = jnp.any(hit, axis=1).astype(jnp.int32)
    share_of = jnp.sum(jnp.where(hit, gate_share, 0.0), axis=1)
    rank = jnp.cumsum(match) - match
    slot = jnp.where(match > 0, rank, -1)
    pick = slot[None, :] == jnp.arange(SLOTS, dtype=jnp.int32)[:, None]
    put = (slot[:, None] == jnp.arange(SLOTS, dtype=jnp.int32)[None, :]).astype(BF)
    place = jnp.arange(tok, dtype=jnp.int32)
    ends = jnp.cumsum(lengths)
    starts = jnp.max(jnp.where(ends[None, :] <= seq_at * tok + place[:, None], ends[None, :], 0), axis=1)
    low_of = starts - (seq_at - REACH) * tok
    low = jnp.sum(jnp.where(pick, low_of[None, :], 0), axis=1)
    high = jnp.sum(jnp.where(pick, place[None, :], 0), axis=1) + REACH * tok
    share = jnp.sum(jnp.where(pick, share_of[None, :], 0.0), axis=1)
    left_share = jnp.tile(share[MAIN:CAP], left_rows // LEFT)
    q_cols = lax.dynamic_slice_in_dim(queries, rep_at * cols, cols, 1)
    q_rows = dot(pick.astype(BF), q_cols).astype(BF)

    spread, share, left_share = call(
        functools.partial(attend_kernel, heads, kv_heads),
        [
            jax.ShapeDtypeStruct((flat, HD), BF),
            jax.ShapeDtypeStruct((MAIN, 1), F32),
            jax.ShapeDtypeStruct((left_rows, 1), F32),
        ],
        flops=4 * heads * SLOTS * 3 * tok * HD,
    )(q_rows, far, near, kv, jnp.tile(low, group)[:, None], jnp.tile(high, group)[:, None], share[:MAIN, None], left_share[:, None])

    gate_w = jnp.transpose(gate_up, (0, 2, 3, 1))
    down_w = jnp.transpose(down_t, (0, 2, 1))
    sib_gate_w = lax.ppermute(gate_w, "seq", sibling)
    sib_down_w = lax.ppermute(down_w, "seq", sibling)
    mine = lax.all_gather(spread, "seq", axis_index_groups=same_core)
    mine, sib_gate_w, sib_down_w, put = lax.optimization_barrier(
        (mine, sib_gate_w, sib_down_w, put)
    )

    full = 2 * hid // HD
    m, n = n_y * MAIN // n_rep, n_y * LEFT // n_rep
    part_rows = 2 * full * m + m // 2 + 2 * n * (full + 1)
    hid_rows = -(-(full * m + m // 2 + n * (full + 1)) // 16) * 16
    parts = call(
        functools.partial(gate_kernel, heads),
        jax.ShapeDtypeStruct((n_rep, part_rows, HD), BF),
        [pltpu.VMEM((n_y * CAP, cols), BF), pltpu.VMEM(gate_w.shape, BF), pltpu.SemaphoreType.DMA],
        flops=8 * n_y * CAP * cols * hid,
        in_hbm=(2, 3),
    )(mine, gate_w, sib_gate_w)
    parts = lax.all_to_all(parts, "rep", split_axis=0, concat_axis=0, tiled=True)
    hidden = call(functools.partial(hidden_kernel, full, m, n), jax.ShapeDtypeStruct((hid_rows, HD), BF))(parts)
    hidden = lax.all_gather(hidden, "rep")
    mine = call(
        functools.partial(down_kernel, heads),
        jax.ShapeDtypeStruct((n_y, flat, HD), BF),
        flops=4 * n_y * CAP * cols * hid,
    )(hidden, down_w, sib_down_w)
    mine = lax.all_to_all(mine, "seq", split_axis=0, concat_axis=0, tiled=True, axis_index_groups=same_core)
    term = call(
        functools.partial(owner_kernel, heads),
        jax.ShapeDtypeStruct((tok, cols), BF),
        [pltpu.VMEM((SLOTS, cols), BF)],
        flops=2 * SLOTS * tok * cols,
    )(mine, put, share, left_share)
    terms = lax.all_to_all(term.reshape(n_exp, tok // n_exp, cols), "exp", split_axis=0, concat_axis=0, tiled=True)
    return jnp.sum(terms.astype(F32), axis=0).astype(BF)


def solution(mesh):
    in_specs = (
        P("seq", None),
        P("seq", None),
        P("seq", None),
        P(),
        P("seq", None),
        P("seq", None),
        P("exp", "rep", None, "seq"),
        P("exp", "rep", "seq"),
    )
    return jax.shard_map(
        per_device, mesh=mesh, in_specs=in_specs, out_specs=P(("seq", "exp"), "rep"), check_vma=False
    )
```

```python
import functools

import jax
import jax.numpy as jnp
from jax import lax
from jax.experimental import pallas as pl
from jax.experimental.pallas import tpu as pltpu
from jax.sharding import PartitionSpec as P

HEADS = 48
KV = 8
HD = 128
REACH = 2
CAP = 34
MAIN = 32
LEFT = CAP - MAIN
SLOTS = 48
BF = jnp.bfloat16
F32 = jnp.float32
NT = (((1,), (1,)), ((), ()))


def dot(a, b):
    return jnp.dot(a, b, preferred_element_type=F32)


def iota(shape, dim):
    return lax.broadcasted_iota(jnp.int32, shape, dim)


def attend_kernel(heads, kv_heads, q_ref, far_ref, near_ref, own_ref, slot_ref, low_ref, share_in, out_ref, put_ref, share_ref, left_ref):
    tok = own_ref.shape[0]
    pick = (slot_ref[...] == iota((SLOTS, tok), 0)).astype(F32)

    def of_slot(row):
        return jnp.sum(pick * row, axis=1, keepdims=True)

    low = of_slot(low_ref[...].astype(F32)).astype(jnp.int32)
    high = of_slot(iota((1, tok), 1).astype(F32)).astype(jnp.int32) + REACH * tok
    share = of_slot(share_in[...])
    share_ref[...] = share[:MAIN]
    odd = iota(left_ref.shape, 0) & 1
    left_ref[...] = jnp.where(odd == 0, share[MAIN : MAIN + 1], share[MAIN + 1 : MAIN + 2])
    same = (iota((tok, tok), 0) == iota((tok, tok), 1)).astype(F32).astype(BF)
    put_ref[...] = lax.dot_general(same, pick.astype(BF), NT, preferred_element_type=F32).astype(BF)
    group = heads // kv_heads
    rows = group * SLOTS
    left_rows = out_ref.shape[0] - heads * MAIN
    keys_in = (REACH + 1) * own_ref.shape[0]
    key_at = iota((rows, keys_in), 1)
    low, high = (jnp.concatenate([bound] * group, 0) for bound in (low, high))
    allowed = (key_at >= low) & (key_at <= high)
    left = jnp.zeros((left_rows, HD), F32)
    for g in range(kv_heads):
        k_cols = slice(g * HD, (g + 1) * HD)
        v_cols = slice((kv_heads + g) * HD, (kv_heads + g + 1) * HD)
        k = jnp.concatenate([ref[:, k_cols] for ref in (far_ref, near_ref, own_ref)], 0)
        v = jnp.concatenate([ref[:, v_cols] for ref in (far_ref, near_ref, own_ref)], 0)
        q = jnp.concatenate([q_ref[:, (g * group + j) * HD : (g * group + j + 1) * HD] for j in range(group)], 0)
        scores = lax.dot_general(q, k, NT, preferred_element_type=F32) * HD ** (-0.5)
        scores = jnp.where(allowed, scores, -jnp.inf)
        weights = jnp.exp(scores - jnp.max(scores, axis=1, keepdims=True))
        probs = (weights / jnp.sum(weights, axis=1, keepdims=True)).astype(BF)
        mixed = dot(probs, v).astype(BF)
        for j in range(group):
            head = g * group + j
            out_ref[head * MAIN : (head + 1) * MAIN, :] = mixed[j * SLOTS : j * SLOTS + MAIN]
        at = iota((left_rows, rows), 0) - g * group * LEFT
        col = iota((left_rows, rows), 1)
        wanted = (at >> 1) * SLOTS + MAIN + (at & 1)
        pick = ((col == wanted) & (at >= 0) & (at < group * LEFT)).astype(F32).astype(BF)
        left = left + dot(pick, mixed)
    out_ref[heads * MAIN :, :] = left.astype(BF)


def left_index(shape, heads, blocks, left_rows, row_dim):
    row, col = iota(shape, row_dim), iota(shape, 1 - row_dim)
    per = blocks * LEFT
    head = row // per
    inside = row - head * per
    return (col == (inside >> 1) * left_rows + head * LEFT + (inside & 1)).astype(F32).astype(BF)


def joined(own, sib, start, stop):
    n = own.shape[0]
    parts = []
    if start < n:
        parts.append(own[start : min(stop, n)])
    if stop > n:
        parts.append(sib[max(start - n, 0) : stop - n])
    return parts[0] if len(parts) == 1 else jnp.concatenate(parts, 0)


def silu_times(gate, up):
    return gate / (1.0 + jnp.exp(-gate)) * up


def gate_kernel(heads, in_ref, own_w_ref, far_w_ref, out_ref, x_ref, sib_w_ref, sem):
    fetch = pltpu.make_async_copy(far_w_ref, sib_w_ref, sem)
    fetch.start()
    blocks, flat, _ = in_ref.shape
    chunks = out_ref.shape[0]
    left_rows = flat - heads * MAIN
    main, extra = blocks * MAIN, blocks * LEFT
    m, n = main // chunks, extra // chunks
    pick = left_index((heads * extra, blocks * left_rows), heads, blocks, left_rows, 0)
    for h in range(heads):
        x_ref[:main, h * HD : (h + 1) * HD] = in_ref[:, h * MAIN : (h + 1) * MAIN, :].reshape(main, HD)
    left = dot(pick, in_ref[:, heads * MAIN :, :].reshape(blocks * left_rows, HD)).astype(BF)
    for h in range(heads):
        x_ref[main:, h * HD : (h + 1) * HD] = left[h * extra : (h + 1) * extra]
    x = x_ref[...]
    full = 2 * own_w_ref.shape[2] // HD

    def times(*w):
        w = w[0] if len(w) == 1 else jnp.concatenate(w, 0)
        return lax.dot_general(x, w, NT, preferred_element_type=F32)

    def units(part, start, stop):
        return joined(own_w_ref.at[0, part], sib_w_ref.at[0, part], start, stop)

    tiles = [[], []]
    for t in range(0, full - 1, 2):
        if t == 2:
            fetch.wait()
        for part in range(2):
            both = times(units(part, t * HD, (t + 2) * HD))
            tiles[part] += [both[:, :HD], both[:, HD:]]
    both = times(*(units(part, (full - 1) * HD, full * HD) for part in range(2)))
    tiles[0].append(both[:, :HD])
    tiles[1].append(both[:, HD:])
    rest = [units(part, full * HD, full * HD + HD // 4) for part in range(2)]
    rest = times(*rest, *rest)
    tiles = tiles[0] + tiles[1]
    packed = 2 * full * m + m // 2
    stack = jnp.concatenate([t[main:] for t in tiles + [rest]], 0).astype(BF)
    per = out_ref.shape[1] - packed
    row, col = iota((chunks * per, stack.shape[0]), 0), iota((chunks * per, stack.shape[0]), 1)
    chunk = row // per
    inside = row - chunk * per
    t, up, i = inside // (2 * n), (inside // n) & 1, inside & (n - 1)
    wanted = jnp.where(t < full, (up * full + t) * extra, jnp.where(up == 0, 2 * full * extra, -stack.shape[0]))
    order = (col == wanted + chunk * n + i).astype(F32).astype(BF)
    left = dot(order, stack).astype(BF)
    first = iota((m // 2, HD), 1) < HD // 2
    for j in range(chunks):
        for k, tile in enumerate(tiles):
            out_ref[j, k * m : (k + 1) * m, :] = tile[j * m : (j + 1) * m].astype(BF)
        pair = jnp.where(first, rest[j * m : j * m + m // 2], rest[j * m + m // 2 : (j + 1) * m])
        out_ref[j, 2 * full * m : packed, :] = pair.astype(BF)
        out_ref[j, packed:, :] = left[j * per : (j + 1) * per]


def hidden_kernel(full, m, n, in_ref, out_ref):
    both = sum(in_ref[i].astype(F32) for i in range(in_ref.shape[0]))
    tall, packed = full * m, 2 * full * m + m // 2
    quarter = HD // 4

    def rest(x):
        return silu_times(x, pltpu.roll(x, HD - quarter, 1))

    main = silu_times(both[:tall], both[tall : 2 * tall])
    pair = both[2 * tall : packed]
    pair = jnp.where((iota(pair.shape, 1) & (2 * quarter - 1)) < quarter, rest(pair), 0.0)
    left = both[packed : packed + 2 * n * full]
    left = silu_times(left, pltpu.roll(left, left.shape[0] - n, 0))
    last = both[packed + 2 * n * full :]
    last = jnp.where(iota(last.shape, 1) < quarter, rest(last), 0.0)
    left = jnp.concatenate([left, last], 0).astype(BF)
    rows = out_ref.shape[0] - tall - m // 2
    row, col = iota((rows, left.shape[0]), 0), iota((rows, left.shape[0]), 1)
    pick = ((col == row // n * 2 * n + (row & (n - 1))) & (row < n * (full + 1))).astype(F32).astype(BF)
    out_ref[:tall, :] = main.astype(BF)
    out_ref[tall : tall + m // 2, :] = pair.astype(BF)
    out_ref[tall + m // 2 :, :] = dot(pick, left).astype(BF)


def down_kernel(heads, hid_ref, own_w_ref, sib_w_ref, out_ref):
    blocks, flat, _ = out_ref.shape
    chunks = hid_ref.shape[0]
    left_rows = flat - heads * MAIN
    main, extra = blocks * MAIN, blocks * LEFT
    m, n = main // chunks, extra // chunks
    put = left_index((blocks * left_rows, heads * extra), heads, blocks, left_rows, 1)
    full = 2 * own_w_ref.shape[1] // HD
    tall = full * m
    rest_rows = hid_ref.shape[1] - tall - m // 2
    tiles = [jnp.concatenate([hid_ref[j, t * m : (t + 1) * m, :] for j in range(chunks)], 0) for t in range(full)]
    first = iota((m // 2, HD), 1) < HD // 2
    pairs = []
    for j in range(chunks):
        pair = hid_ref[j, tall : tall + m // 2, :].astype(F32)
        pairs += [jnp.where(first, pair, 0.0), jnp.where(first, 0.0, pair)]
    tiles.append(jnp.concatenate(pairs, 0).astype(BF))
    stack = jnp.concatenate([hid_ref[j, tall + m // 2 :, :] for j in range(chunks)], 0)
    shape = ((full + 1) * extra, stack.shape[0])
    row, col = iota(shape, 0), iota(shape, 1)
    t = row // extra
    inside = row - t * extra
    order = (col == inside // n * rest_rows + t * n + (inside & (n - 1))).astype(F32).astype(BF)
    left = dot(order, stack).astype(BF)
    hidden = [jnp.concatenate([tile, left[t * extra : (t + 1) * extra]], 0) for t, tile in enumerate(tiles)]

    def units(start, stop):
        return joined(own_w_ref.at[0], sib_w_ref.at[0], start, stop)

    out = None
    for t in range(0, full + 1, 2):
        if t + 2 <= full:
            w = units(t * HD, (t + 2) * HD)
        else:
            w = jnp.concatenate([units(t * HD, full * HD)] + [units(full * HD, full * HD + HD // 4)] * 4, 0)
        term = dot(jnp.concatenate(hidden[t : t + 2], 1), w)
        out = term if out is None else out + term
    out = out.astype(BF)
    for h in range(heads):
        out_ref[:, h * MAIN : (h + 1) * MAIN, :] = out[:main, h * HD : (h + 1) * HD].reshape(blocks, MAIN, HD)
    stack = jnp.concatenate([out[main:, h * HD : (h + 1) * HD] for h in range(heads)], 0)
    out_ref[:, heads * MAIN :, :] = dot(put, stack).astype(BF).reshape(blocks, left_rows, HD)


def owner_kernel(heads, in_ref, put_ref, share_ref, left_share_ref, out_ref, x_ref):
    flat = in_ref.shape[1]
    left_rows = flat - heads * MAIN
    total = sum(in_ref[y].astype(F32) for y in range(in_ref.shape[0]))
    share = share_ref[...]
    left = (total[heads * MAIN :] * left_share_ref[...]).astype(BF)
    rest = SLOTS - MAIN
    row, col = iota((heads * rest, left_rows), 0), iota((heads * rest, left_rows), 1)
    head = row // rest
    inside = row - head * rest
    pick = ((col == head * LEFT + inside) & (inside < LEFT)).astype(F32).astype(BF)
    left = dot(pick, left).astype(BF)
    for h in range(heads):
        cols = slice(h * HD, (h + 1) * HD)
        x_ref[:MAIN, cols] = (total[h * MAIN : (h + 1) * MAIN] * share).astype(BF)
        x_ref[MAIN:, cols] = left[h * rest : (h + 1) * rest]
    out_ref[...] = dot(put_ref[...], x_ref[...]).astype(BF)


def call(kernel, shapes, scratch=(), flops=0, moved=0, in_hbm=None):
    spaces = {}
    if in_hbm is not None:
        spaces["in_specs"] = [pl.BlockSpec(memory_space=pl.ANY if at == in_hbm[0] else pltpu.VMEM) for at in range(in_hbm[1])]
    return pl.pallas_call(
        kernel,
        **spaces,
        out_shape=shapes,
        scratch_shapes=list(scratch),
        compiler_params=pltpu.CompilerParams(vmem_limit_bytes=12 * 1024 * 1024),
        cost_estimate=pl.CostEstimate(flops=flops, bytes_accessed=moved, transcendentals=0),
    )


def per_device(queries, keys, values, lengths, expert_ids, gate_share, gate_up, down_t):
    n_seq, n_exp, n_rep = (lax.axis_size(a) for a in ("seq", "exp", "rep"))
    tok = queries.shape[0]
    cols = gate_up.shape[1]
    hid = gate_up.shape[3]
    heads, kv_heads = cols // HD, KV // n_rep
    group = heads // kv_heads
    n_y = n_seq // 2
    left_rows = -(-heads * LEFT // 16) * 16
    flat = heads * MAIN + left_rows
    seq_at, exp_at, rep_at = (lax.axis_index(a) for a in ("seq", "exp", "rep"))
    same_core = [[2 * y + c for y in range(n_y)] for c in range(2)]
    sibling = [(i, i ^ 1) for i in range(n_seq)]

    kv_cols = kv_heads * HD
    kv = jnp.concatenate(
        [
            lax.dynamic_slice_in_dim(keys, rep_at * kv_cols, kv_cols, 1),
            lax.dynamic_slice_in_dim(values, rep_at * kv_cols, kv_cols, 1),
        ],
        1,
    )
    far = lax.ppermute(kv, "seq", [(i, (i + 2) % n_seq) for i in range(n_seq)])
    near = lax.ppermute(kv, "seq", [(i, (i + 1) % n_seq) for i in range(n_seq)])

    hit = expert_ids == exp_at
    match = jnp.any(hit, axis=1).astype(jnp.int32)
    share_of = jnp.sum(jnp.where(hit, gate_share, 0.0), axis=1)
    rank = jnp.cumsum(match) - match
    slot = jnp.where(match > 0, rank, -1)
    pick = slot[None, :] == jnp.arange(SLOTS, dtype=jnp.int32)[:, None]
    place = jnp.arange(tok, dtype=jnp.int32)
    ends = jnp.cumsum(lengths)
    starts = jnp.max(jnp.where(ends[None, :] <= seq_at * tok + place[:, None], ends[None, :], 0), axis=1)
    low_of = starts - (seq_at - REACH) * tok
    q_cols = lax.dynamic_slice_in_dim(queries, rep_at * cols, cols, 1)
    q_rows = dot(pick.astype(BF), q_cols).astype(BF)

    spread, put, share, left_share = call(
        functools.partial(attend_kernel, heads, kv_heads),
        [
            jax.ShapeDtypeStruct((flat, HD), BF),
            jax.ShapeDtypeStruct((tok, SLOTS), BF),
            jax.ShapeDtypeStruct((MAIN, 1), F32),
            jax.ShapeDtypeStruct((left_rows, 1), F32),
        ],
        flops=4 * heads * SLOTS * 3 * tok * HD,
    )(q_rows, far, near, kv, slot[None], low_of[None], share_of[None])

    gate_w = jnp.transpose(gate_up, (0, 2, 3, 1))
    down_w = jnp.transpose(down_t, (0, 2, 1))
    sib_gate_w = lax.ppermute(gate_w, "seq", sibling)
    sib_down_w = lax.ppermute(down_w, "seq", sibling)
    mine = lax.all_gather(spread, "seq", axis_index_groups=same_core)
    mine, sib_gate_w, sib_down_w = lax.optimization_barrier((mine, sib_gate_w, sib_down_w))

    full = 2 * hid // HD
    m, n = n_y * MAIN // n_rep, n_y * LEFT // n_rep
    part_rows = 2 * full * m + m // 2 + 2 * n * (full + 1)
    hid_rows = -(-(full * m + m // 2 + n * (full + 1)) // 16) * 16
    parts = call(
        functools.partial(gate_kernel, heads),
        jax.ShapeDtypeStruct((n_rep, part_rows, HD), BF),
        [pltpu.VMEM((n_y * CAP, cols), BF), pltpu.VMEM(gate_w.shape, BF), pltpu.SemaphoreType.DMA],
        flops=8 * n_y * CAP * cols * hid,
        in_hbm=(2, 3),
    )(mine, gate_w, sib_gate_w)
    parts = lax.all_to_all(parts, "rep", split_axis=0, concat_axis=0, tiled=True)
    hidden = call(functools.partial(hidden_kernel, full, m, n), jax.ShapeDtypeStruct((hid_rows, HD), BF))(parts)
    hidden = lax.all_gather(hidden, "rep")
    mine = call(
        functools.partial(down_kernel, heads),
        jax.ShapeDtypeStruct((n_y, flat, HD), BF),
        flops=4 * n_y * CAP * cols * hid,
    )(hidden, down_w, sib_down_w)
    mine = lax.all_to_all(mine, "seq", split_axis=0, concat_axis=0, tiled=True, axis_index_groups=same_core)
    term = call(
        functools.partial(owner_kernel, heads),
        jax.ShapeDtypeStruct((tok, cols), BF),
        [pltpu.VMEM((SLOTS, cols), BF)],
        flops=2 * SLOTS * tok * cols,
    )(mine, put, share, left_share)
    terms = lax.all_to_all(term.reshape(n_exp, tok // n_exp, cols), "exp", split_axis=0, concat_axis=0, tiled=True)
    return jnp.sum(terms.astype(F32), axis=0).astype(BF)


def solution(mesh):
    in_specs = (
        P("seq", None),
        P("seq", None),
        P("seq", None),
        P(),
        P("seq", None),
        P("seq", None),
        P("exp", "rep", None, "seq"),
        P("exp", "rep", "seq"),
    )
    return jax.shard_map(
        per_device, mesh=mesh, in_specs=in_specs, out_specs=P(("seq", "exp"), "rep"), check_vma=False
    )
```
